256 devices in a mesh: grp: 8 (over y, core), dev: 32 (over z, x).
Axes of the slice: x: 4, y: 4, z: 8, core: 2. Of those that a mesh axis runs over, the one named last changes fastest.
Arguments:
- sample_rows: bfloat16 [262144, 768], P(('grp', 'dev'))
- row_cell: int32 [262144], P(('grp', 'dev')), may hold values from 0 to 65535, as said below
- tile_rows: int32 [512], P(('grp', 'dev')), may hold values from 0 to 512, as said below
- centroids: bfloat16 [65536, 768], P(('grp', 'dev')), may hold values from -4 to 4
- rotation: bfloat16 [768, 768], replicated, may hold values from -0.21875 to 0.21875
- codebooks: bfloat16 [96, 8, 256], replicated, may hold values from -5 to 5
Outputs:
- cross_cov: float32 [768, 768], replicated
- code_sums: float32 [96, 8, 256], replicated
- code_mass: float32 [96, 256], replicated
The draws below stay inside these ranges and needn't reach their ends.
Inputs may be any that keep to these rules, and one draw needn't show every extreme that they name: `row_cell`: every row's cell is owned by the device that holds the row: cell // 256 equals row // 1024; cells are unevenly filled. `tile_rows`: the first tile of every device is full; others hold any number of live rows.
All inputs are finite; a program needn't handle non-finite values.
Results may differ from the reference program's by a relative error of at most 0.0024.
Values may be sent and summed in bfloat16 or wider, within the bound.
A program may use at most 64 MiB of HBM per device.

```python
import jax
import jax.numpy as jnp
from jax import lax

D = 768
SUBS = 96
SUB_DIM = 8
CODES = 256
SUB_BLOCK = 8
TILE = 512
SLOTS = 2
CELLS_DEV = 256
ROWS = 262144
CELLS = 65536
TILE_COUNT = 512


def draw_sample_rows(key, part):
    key = jax.random.fold_in(key, 5)
    return jax.random.normal(key, (ROWS, D), jnp.float32).astype(jnp.bfloat16)


def draw_row_cell(key, part):
    key = jax.random.fold_in(key, 11)
    ka, kb = jax.random.split(key)
    first = jax.random.randint(ka, (ROWS,), 0, CELLS_DEV)
    second = jax.random.randint(kb, (ROWS,), 0, CELLS_DEV)
    local = jnp.minimum(first, second)
    per_dev = SLOTS * TILE
    place = jnp.arange(ROWS) % per_dev
    local = jnp.where(place == 0, 0, jnp.where(place == per_dev - 1, CELLS_DEV - 1, local))
    return (jnp.arange(ROWS) // per_dev * CELLS_DEV + local).astype(jnp.int32)


def draw_tile_rows(key, part):
    key = jax.random.fold_in(key, 17)
    ka, kb = jax.random.split(key)
    amount = jax.random.randint(ka, (TILE_COUNT,), 0, TILE + 1)
    keep = jax.random.randint(kb, (TILE_COUNT,), 0, 2)
    slot = jnp.arange(TILE_COUNT) % SLOTS
    return jnp.where(slot == 0, TILE, amount * keep).astype(jnp.int32)


def block_levels(key, shape, cuts, smallest, top_value):
    gain = 1.0
    for dim, blocks in cuts:
        heights = jax.random.uniform(jax.random.fold_in(jax.random.fold_in(key, 6), dim), (blocks,), jnp.float32, smallest / len(cuts), top_value / len(cuts))
        gain = gain * jnp.repeat(jnp.exp(heights), shape[dim] // blocks).reshape((-1,) + (1,) * (len(shape) - 1 - dim))
    return gain


def centred(rng, shape, width, most, pieces=(), held_as=jnp.bfloat16):
    result = jax.random.normal(rng, shape, jnp.float32) * width
    if len(pieces) > 0:
        result = block_levels(rng, shape, pieces, -0.22, 0.18) * result
    return jnp.clip(result, min=-most, max=most).astype(held_as)


def setup_inputs(seed: int = 0) -> dict:
    arg_keys = jax.random.split(jax.random.key(seed), 7)
    return {
        "sample_rows": draw_sample_rows(jax.random.fold_in(arg_keys[6], 71), 0),
        "row_cell": draw_row_cell(jax.random.fold_in(arg_keys[6], 71), 0),
        "tile_rows": draw_tile_rows(jax.random.fold_in(arg_keys[6], 71), 0),
        "centroids": centred(arg_keys[3], (CELLS, D), 0.5, 4.0, ((0, 256),)),
        "rotation": centred(arg_keys[4], (D, D), D ** -0.5, 0.21875),
        "codebooks": centred(arg_keys[5], (SUBS, SUB_DIM, CODES), 1.0, 5.0),
    }


BETA = 0.5


def tile_terms(rows, cent, count, rotation, codebooks):
    tile = rows.shape[0]
    valid = (jnp.arange(tile) < count).astype(jnp.float32)
    resid = (rows.astype(jnp.float32) - cent.astype(jnp.float32)).astype(jnp.bfloat16)
    rotated = jnp.dot(resid, rotation, preferred_element_type=jnp.float32).astype(jnp.bfloat16)
    nblk = SUBS // SUB_BLOCK
    ys = rotated.reshape(tile, nblk, SUB_BLOCK, SUB_DIM).transpose(1, 0, 2, 3)
    cbs = codebooks.reshape(nblk, SUB_BLOCK, SUB_DIM, CODES)

    def step(carry, pair):
        yb, cb = pair
        yf = yb.astype(jnp.float32)
        cf = cb.astype(jnp.float32)
        cross = jnp.einsum('rmd,mdk->rmk', yf, cf)
        ysq = jnp.sum(yf * yf, -1)[:, :, None]
        csq = jnp.sum(cf * cf, 1)[None]
        score = -BETA * (ysq - 2.0 * cross + csq)
        weight = (jax.nn.softmax(score, -1) * valid[:, None, None]).astype(jnp.bfloat16)
        wf = weight.astype(jnp.float32)
        sums = jnp.einsum('rmk,rmd->mdk', wf, yf)
        mass = jnp.sum(wf, 0)
        approx = jnp.einsum('rmk,mdk->rmd', wf, cf).astype(jnp.bfloat16)
        return carry, (sums, mass, approx)

    unused, (sums, mass, approx) = lax.scan(step, jnp.float32(0.0), (ys, cbs))
    approx = approx.transpose(1, 0, 2, 3).reshape(tile, D)
    cov = jnp.dot(resid.T, approx, preferred_element_type=jnp.float32)
    return cov, sums.reshape(SUBS, SUB_DIM, CODES), mass.reshape(SUBS, CODES)


def reference(sample_rows, row_cell, tile_rows, centroids, rotation, codebooks):
    tiles = sample_rows.reshape(TILE_COUNT, TILE, D)
    cells = row_cell.reshape(TILE_COUNT, TILE)

    def step(carry, item):
        rows, cell, count = item
        cent = jnp.take(centroids, cell, axis=0)
        cov, sums, mass = tile_terms(rows, cent, count, rotation, codebooks)
        return (carry[0] + cov, carry[1] + sums, carry[2] + mass), None

    init = (jnp.zeros((D, D), jnp.float32), jnp.zeros((SUBS, SUB_DIM, CODES), jnp.float32), jnp.zeros((SUBS, CODES), jnp.float32))
    (cov, sums, mass), unused = lax.scan(step, init, (tiles, cells, tile_rows))
    total = float(ROWS)
    return cov / total, sums * (CODES / total), mass * (CODES / total)
```

```python
import functools
from jax.sharding import PartitionSpec as P
import jax
import jax.numpy as jnp
from jax import lax
import jax.experimental.pallas as pl, jax.experimental.pallas.tpu as pltpu
bf=jnp.bfloat16; f32=jnp.float32
LOG2E=1.4426950408889634
NT=(((1,),(1,)),((),()))
TN=(((0,),(0,)),((),()))
R=1024; D=768; K=256; G=6; GM=16
CH=256

def prep(rows,cell,cent,rot,cb,resid,yx,yT):
    for b in range(R//256):
        rs=slice(b*256,(b+1)*256)
        oh=(lax.broadcasted_iota(jnp.int32,(256,256),0)==cell[0:1,rs]).astype(bf)
        c=lax.dot_general(oh,cent[...],TN,preferred_element_type=f32)
        rr=(rows[rs,:].astype(f32)-c).astype(bf)
        resid[rs,:]=rr
        y=jnp.dot(rr,rot[...],preferred_element_type=f32)
        yT[:,rs]=y.T.astype(bf)
        yb=y.astype(bf)
        for g in range(G):
            yx[g,rs,0:128]=yb[:,g*128:(g+1)*128]
            yx[g,rs,128:256]=jnp.ones((256,128),bf)

def score_mat(c, j):
    row=lax.broadcasted_iota(jnp.int32,(128,256),0)
    rep=jnp.concatenate([c]*16,axis=0)
    top=jnp.where(row//8==j,rep,0.0)
    bias=-0.5*jnp.sum(c*c,axis=0,keepdims=True)
    h=bias.astype(bf).astype(f32); r1=bias-h; m=r1.astype(bf).astype(f32); l=r1-m
    bot=jnp.where(row==0,h,jnp.where(row==1,m,jnp.where(row==2,l,0.0)))
    return jnp.concatenate([top,bot],axis=0).astype(bf)

def stage1(g,j,cb,yx,E,mode):
    c=cb[g*GM+j].astype(f32)
    A=score_mat(c,j)
    for ch in range(R//CH):
        rs=slice(ch*CH,(ch+1)*CH)
        s=jnp.dot(yx[g,rs,:],A,preferred_element_type=f32)
        if mode=="max":
            s=s-jnp.max(s,axis=1,keepdims=True)
        E[rs,:]=jnp.exp2(s*LOG2E).astype(bf)

def stage2(g,j,cb,yT,E,valid,apT,sums,mass,held):
    c=cb[g*GM+j].astype(f32)
    one=(lax.broadcasted_iota(jnp.int32,(8,256),0)==0).astype(f32)
    caug=jnp.concatenate([c,one],axis=0).astype(bf)
    q=lax.dot_general(caug,E[...],NT,preferred_element_type=f32)
    inv=valid/q[8:9,:]
    ap=q[0:8,:]*inv
    r0=pl.multiple_of(g*128+(j//2)*16,16)
    y16=yT[pl.ds(r0,16),:].astype(f32)
    ym=y16[(j%2)*8:(j%2)*8+8,:]
    rowid=lax.broadcasted_iota(jnp.int32,(8,R),0)
    L=jnp.concatenate([ym*inv,jnp.where(rowid==0,inv,0.0)],axis=0).astype(bf)
    o=jnp.dot(L,E[...],preferred_element_type=f32)
    sums[g*GM+j]=o[0:8,:]
    held.append((ap,o[8:9,:]))
    if j%2==1:
        apT[pl.ds(r0,16),:]=jnp.concatenate([held[-2][0],held[-1][0]],axis=0).astype(bf)
    if j%8==7:
        mass[pl.ds(pl.multiple_of(g*16+j-7,8),8),:]=jnp.concatenate([h[1] for h in held[-8:]],axis=0)

def kernel(mode,tiles,rows,cell,cent,rot,cb,cov,sums,mass,resid,yx,yT,apT,*Es):
    prep(rows,cell,cent,rot,cb,resid,yx,yT)
    pos=lax.broadcasted_iota(jnp.int32,(1,R),1)
    valid=(pos<jnp.where(pos<512,tiles[0],512+tiles[1])).astype(f32)
    NE=len(Es)
    def body(g,_):
        held=[]
        stage1(g,0,cb,yx,Es[0],mode)
        for j in range(GM):
            if j+1<GM: stage1(g,j+1,cb,yx,Es[(j+1)%NE],mode)
            stage2(g,j,cb,yT,Es[j%NE],valid,apT,sums,mass,held)
        return 0
    lax.fori_loop(0,G,body,0)
    for i in range(3):
        cs=slice(i*256,(i+1)*256)
        cov[:,cs]=lax.dot_general(resid[...],apT[cs,:],(((0,),(1,)),((),())),preferred_element_type=f32)

def run(mode,NE,tiles,rows,cell,cent,rot,cb):
    V=pl.BlockSpec(memory_space=pltpu.VMEM)
    S=jax.ShapeDtypeStruct
    return pl.pallas_call(functools.partial(kernel,mode),
      out_shape=(S((D,D),f32),S((96,8,256),f32),S((96,256),f32)),
      in_specs=[pl.BlockSpec(memory_space=pltpu.SMEM)]+[V]*5,out_specs=(V,V,V),
      scratch_shapes=[pltpu.VMEM((R,D),bf),pltpu.VMEM((G,R,256),bf),pltpu.VMEM((D,R),bf),pltpu.VMEM((D,R),bf)]+[pltpu.VMEM((R,256),bf)]*NE,
      compiler_params=pltpu.CompilerParams(vmem_limit_bytes=60*2**20))(tiles,rows,cell,cent,rot,cb)


def per_device(sample_rows, row_cell, tile_rows, centroids, rotation, codebooks):
    n_dev = lax.axis_size("dev")
    n_grp = lax.axis_size("grp")
    device = lax.axis_index("grp") * n_dev + lax.axis_index("dev")
    cell = (row_cell - device * centroids.shape[0]).reshape(1, R)
    cov, sums, mass = run("max", 2, tile_rows, sample_rows, cell, centroids, rotation, codebooks)
    cov, sums, mass = lax.psum((cov, sums, mass), ("grp", "dev"))
    total = float(R * n_dev * n_grp)
    return cov / total, sums * (K / total), mass * (K / total)


def solution(mesh):
    placed = (P(("grp", "dev"), None), P(("grp", "dev")), P(("grp", "dev")), P(("grp", "dev"), None), P(), P())
    return jax.shard_map(per_device, mesh=mesh, in_specs=placed, out_specs=(P(), P(), P()), check_vma=False)
```

```python
import functools
from jax.sharding import PartitionSpec as P
import jax
import jax.numpy as jnp
from jax import lax
import jax.experimental.pallas as pl, jax.experimental.pallas.tpu as pltpu
bf=jnp.bfloat16; f32=jnp.float32
LOG2E=1.4426950408889634
NT=(((1,),(1,)),((),()))
TN=(((0,),(0,)),((),()))
R=1024; D=768; K=256; G=6; GM=16
CH=256

def prep(rows,cell,cent,rot,residT,yx,yT):
    for b in range(R//256):
        rs=slice(b*256,(b+1)*256)
        oh=(lax.broadcasted_iota(jnp.int32,(256,256),0)==cell[0:1,rs]).astype(bf)
        c=lax.dot_general(oh,cent[...],TN,preferred_element_type=f32)
        rr=(rows[rs,:].astype(f32)-c).astype(bf)
        residT[:,rs]=rr.astype(f32).T.astype(bf)
        y=jnp.dot(rr,rot[...],preferred_element_type=f32)
        yT[:,rs]=y.T.astype(bf)
        yb=y.astype(bf)
        for g in range(G):
            yx[g,rs,0:128]=yb[:,g*128:(g+1)*128]
            yx[g,rs,128:256]=jnp.ones((256,128),bf)

def score_mat(c, j):
    row=lax.broadcasted_iota(jnp.int32,(128,256),0)
    rep=jnp.concatenate([c]*16,axis=0)
    top=jnp.where(row//8==j,rep,0.0)
    bias=-0.5*jnp.sum(c*c,axis=0,keepdims=True)
    h=bias.astype(bf).astype(f32); r1=bias-h; m=r1.astype(bf).astype(f32); l=r1-m
    bot=jnp.where(row==0,h,jnp.where(row==1,m,jnp.where(row==2,l,0.0)))
    return jnp.concatenate([top,bot],axis=0).astype(bf)

def stage1(g,j,cb,yx,E,mode):
    c=cb[g*GM+j].astype(f32)
    A=score_mat(c,j)
    for ch in range(R//CH):
        rs=slice(ch*CH,(ch+1)*CH)
        s=jnp.dot(yx[g,rs,:],A,preferred_element_type=f32)
        if mode=="max":
            s=s-jnp.max(s,axis=1,keepdims=True)
        E[rs,:]=jnp.exp2(s*LOG2E).astype(bf)


NX=4; NY=4; NZ=8


def stage2(g,j,cb,yT,E,valid,apT,part,held):
    c=cb[g*GM+j].astype(f32)
    one=(lax.broadcasted_iota(jnp.int32,(8,256),0)==0).astype(f32)
    caug=jnp.concatenate([c,one],axis=0).astype(bf)
    q=lax.dot_general(caug,E[...],NT,preferred_element_type=f32)
    inv=valid/q[8:9,:]
    ap=q[0:8,:]*inv
    r0=pl.multiple_of(g*128+(j//2)*16,16)
    ym=yT[pl.ds(r0,16),:].astype(f32)[(j%2)*8:(j%2)*8+8,:]
    rowid=lax.broadcasted_iota(jnp.int32,(8,R),0)
    L=jnp.concatenate([ym*inv,jnp.where(rowid==0,inv,0.0)],axis=0).astype(bf)
    o=jnp.dot(L,E[...],preferred_element_type=f32)
    cc,hh,aa=j//8,(j//4)%2,j%4
    part[g,cc,hh,aa*8+6]=o[0:8,0:128]
    part[g,cc,hh,aa*8+7]=o[0:8,128:256]
    held.append((ap,o[8:9,:]))
    if j%2==1:
        apT[(j//2)*16:(j//2)*16+16,:]=jnp.concatenate([held[-2][0],held[-1][0]],axis=0).astype(bf)
    if j%8==7:
        mm=jnp.concatenate([h[1] for h in held[-8:]],axis=0)
        part[g,cc,0,32]=mm[:,0:128]
        part[g,cc,1,32]=mm[:,128:256]


def covariance(g,residT,apT,part):
    for cc in range(2):
        for hh in range(2):
            i0=cc*384+hh*192
            v=lax.dot_general(residT[i0:i0+192,:],apT[...],NT,preferred_element_type=f32)
            v=v.reshape(4,6,8,128)
            for aa in range(4):
                part[g,cc,hh,aa*8:aa*8+6]=v[aa]


def kernel(tiles,rows,cell,cent,rot,cb,cov,sums,mass,
           residT,yx,yT,apT,E0,E1,part,rc,sa,ra,sz,rz,rl,out,
           s_core,r_core,s_a,r_a,s_z,r_z,s_l,r_l,s_gz,r_gz,s_ga,r_ga,s_gc,r_gc):
    grp=lax.axis_index("grp"); dev=lax.axis_index("dev")
    yy=grp//2; c=lax.rem(grp,2); zz=dev//NX; xx=lax.rem(dev,NX)
    sib=(yy*2+1-c,dev)
    def at_y(t): return (t*2+c,dev)
    def at_x(t): return (grp,zz*NX+t)
    def at_z(t): return (grp,t*NX+xx)
    first=((yy,at_y),(xx,at_x)); last=((xx,at_x),(yy,at_y))

    barrier=pltpu.get_barrier_semaphore()
    peers=[sib]+[at_y(lax.rem(yy+k,NY)) for k in range(1,NY)]+[at_x(lax.rem(xx+k,NX)) for k in range(1,NX)]+[at_z(lax.rem(zz+k,NZ)) for k in range(1,NZ)]
    for p in peers:
        pl.semaphore_signal(barrier,inc=1,device_id=p,device_id_type=pl.DeviceIdType.MESH)

    def copy(src,dst,ss,rs,to):
        return pltpu.make_async_remote_copy(src_ref=src,dst_ref=dst,send_sem=ss,recv_sem=rs,device_id=to,device_id_type=pl.DeviceIdType.MESH)

    def step(k,g):
        if k==0:
            copy(part.at[g,1-c],rc.at[g],s_core.at[0],r_core.at[g],sib).start()
        if k==1:
            copy(rc.at[g],rc.at[g],s_core.at[0],r_core.at[g],sib).wait_recv()
            for h in range(2):
                me,at=first[h]
                tot=part[g,c,h]+rc[g,h]
                for a in range(4):
                    sa[g,h,a,0:8]=tot[a*8:a*8+8]
                    sa[g,h,a,8]=tot[32]
                for kk in range(1,4):
                    a=lax.rem(me+kk,4)
                    copy(sa.at[g,h,a],ra.at[g,h,me],s_a.at[0],r_a.at[g,h],at(a)).start()
                ra[g,h,me]=sa[g,h,me]
        if k==2:
            for h in range(2):
                me,at=first[h]
                copy(sa.at[g,h,0:3],ra.at[g,h,0:3],s_a.at[0],r_a.at[g,h],sib).wait_recv()
                tot=(ra[g,h,0]+ra[g,h,1])+(ra[g,h,2]+ra[g,h,3])
                for z in range(NZ):
                    sz[g,h,z,0]=tot[z]
                    sz[g,h,z,1]=tot[8]
                for kk in range(1,NZ):
                    z=lax.rem(zz+kk,NZ)
                    copy(sz.at[g,h,z],rz.at[g,h,zz],s_z.at[0],r_z.at[g,h],at_z(z)).start()
                rz[g,h,zz]=sz[g,h,zz]
        if k==3:
            for h in range(2):
                me,at=last[h]
                copy(sz.at[g,h,0:7],rz.at[g,h,0:7],s_z.at[0],r_z.at[g,h],sib).wait_recv()
                t=[rz[g,h,z] for z in range(NZ)]
                rl[g,h,me]=((t[0]+t[1])+(t[2]+t[3]))+((t[4]+t[5])+(t[6]+t[7]))
                for kk in range(1,4):
                    a=lax.rem(me+kk,4)
                    copy(rl.at[g,h,me],rl.at[g,h,me],s_l.at[0],r_l.at[g,h],at(a)).start()
        if k==4:
            for h in range(2):
                me,_=first[h]
                copy(rl.at[g,h,0:3],rl.at[g,h,0:3],s_l.at[0],r_l.at[g,h],sib).wait_recv()
                tot=(rl[g,h,0]+rl[g,h,1])+(rl[g,h,2]+rl[g,h,3])
                mine=out.at[g,c,h,me*8+zz]
                mine[...]=tot[0]
                out[g,c,h,32]=tot[1]
                for kk in range(1,NZ):
                    z=lax.rem(zz+kk,NZ)
                    copy(mine,mine,s_gz.at[0],r_gz.at[g,h],at_z(z)).start()
        if k==5:
            for h in range(2):
                me,at=first[h]
                copy(out.at[g,c,h,0:7],out.at[g,c,h,0:7],s_gz.at[0],r_gz.at[g,h],sib).wait_recv()
                mine=out.at[g,c,h,pl.ds(me*8,8)]
                for kk in range(1,4):
                    a=lax.rem(me+kk,4)
                    copy(mine,mine,s_ga.at[0],r_ga.at[g,h],at(a)).start()
        if k==6:
            for h in range(2):
                copy(out.at[g,c,h,0:24],out.at[g,c,h,0:24],s_ga.at[0],r_ga.at[g,h],sib).wait_recv()
            copy(out.at[g,c],out.at[g,c],s_gc.at[0],r_gc.at[g],sib).start()
        if k==7:
            copy(out.at[g,1-c],out.at[g,1-c],s_gc.at[0],r_gc.at[g],sib).wait_recv()
            for cc in range(2):
                for hh in range(2):
                    for aa in range(4):
                        i0=cc*384+hh*192+aa*48
                        cov[i0:i0+48,pl.ds(pl.multiple_of(g*128,128),128)]=out[g,cc,hh,aa*8:aa*8+6].reshape(48,128)
                        for w in range(2):
                            sums[g*GM+cc*8+hh*4+aa,:,w*128:(w+1)*128]=out[g,cc,hh,aa*8+6+w]
                    mass[pl.ds(pl.multiple_of(g*GM+cc*8,8),8),hh*128:(hh+1)*128]=out[g,cc,hh,32]

    prep(rows,cell,cent,rot,residT,yx,yT)
    pos=lax.broadcasted_iota(jnp.int32,(1,R),1)
    valid=(pos<jnp.where(pos<512,tiles[0],512+tiles[1])).astype(f32)
    pl.semaphore_wait(barrier,len(peers))
    Es=(E0,E1)

    def body(g,_):
        held=[]
        stage1(g,0,cb,yx,E0,"max")
        for j in range(GM):
            if j+1<GM: stage1(g,j+1,cb,yx,Es[(j+1)%2],"max")
            stage2(g,j,cb,yT,Es[j%2],valid,apT,part,held)
            if j==7:
                for k in (1,3,5,7):
                    back=(k+1)//2
                    @pl.when(g>=back)
                    def _(k=k,back=back): step(k,g-back)
        covariance(g,residT,apT,part)
        for k in (0,2,4,6):
            back=k//2
            if back==0: step(0,g)
            else:
                @pl.when(g>=back)
                def _(k=k,back=back): step(k,g-back)
        return 0
    lax.fori_loop(0,G,body,0)
    for sp in range(2*G,2*G+7):
        for k in range(8):
            if (sp-1-k)%2==0 and 0<=(sp-1-k)//2<G:
                step(k,(sp-1-k)//2)
    copy(rc,rc,s_core.at[0],r_core.at[0],sib).wait_send()
    copy(sa.at[:,:,0:3],ra.at[:,:,0:3],s_a.at[0],r_a.at[0,0],sib).wait_send()
    copy(sz.at[:,:,0:7],rz.at[:,:,0:7],s_z.at[0],r_z.at[0,0],sib).wait_send()
    copy(rl.at[:,:,0:3],rl.at[:,:,0:3],s_l.at[0],r_l.at[0,0],sib).wait_send()
    copy(out.at[:,0,:,0:7],out.at[:,0,:,0:7],s_gz.at[0],r_gz.at[0,0],sib).wait_send()
    copy(out.at[:,0,:,0:24],out.at[:,0,:,0:24],s_ga.at[0],r_ga.at[0,0],sib).wait_send()
    copy(out.at[:,0],out.at[:,0],s_gc.at[0],r_gc.at[0],sib).wait_send()


def run(tiles,rows,cell,cent,rot,cb):
    V=pl.BlockSpec(memory_space=pltpu.VMEM)
    S=jax.ShapeDtypeStruct
    T=lambda *n: pltpu.VMEM(n+(8,128),f32)
    DS=pltpu.SemaphoreType.DMA
    return pl.pallas_call(kernel,
      out_shape=(S((D,D),f32),S((96,8,256),f32),S((96,256),f32)),
      in_specs=[pl.BlockSpec(memory_space=pltpu.SMEM)]+[V]*5,out_specs=(V,V,V),
      scratch_shapes=[pltpu.VMEM((D,R),bf),pltpu.VMEM((G,R,256),bf),pltpu.VMEM((D,R),bf),pltpu.VMEM((128,R),bf),
                      pltpu.VMEM((R,256),bf),pltpu.VMEM((R,256),bf),
                      T(G,2,2,33),T(G,2,33),T(G,2,4,9),T(G,2,4,9),T(G,2,8,2),T(G,2,8,2),T(G,2,4,2),T(G,2,2,33),
                      DS((1,)),DS((G,)),DS((1,)),DS((G,2)),DS((1,)),DS((G,2)),DS((1,)),DS((G,2)),
                      DS((1,)),DS((G,2)),DS((1,)),DS((G,2)),DS((1,)),DS((G,))],
      compiler_params=pltpu.CompilerParams(vmem_limit_bytes=56*2**20,collective_id=0,has_side_effects=True),
      cost_estimate=pl.CostEstimate(flops=2**34,bytes_accessed=2**23,transcendentals=2**24))(tiles,rows,cell,cent,rot,cb)


def per_device(sample_rows, row_cell, tile_rows, centroids, rotation, codebooks):
    n_dev = lax.axis_size("dev")
    n_grp = lax.axis_size("grp")
    device = lax.axis_index("grp") * n_dev + lax.axis_index("dev")
    cell = (row_cell - device * centroids.shape[0]).reshape(1, R)
    cov, sums, mass = run(tile_rows, sample_rows, cell, centroids, rotation, codebooks)
    total = float(R * n_dev * n_grp)
    return cov / total, sums * (K / total), mass * (K / total)


def solution(mesh):
    placed = (P(("grp", "dev"), None), P(("grp", "dev")), P(("grp", "dev")), P(("grp", "dev"), None), P(), P())
    return jax.shard_map(per_device, mesh=mesh, in_specs=placed, out_specs=(P(), P(), P()), check_vma=False)
```

```python
import functools
import jax
import jax.numpy as jnp
from jax import lax
from jax.sharding import PartitionSpec as P
import jax.experimental.pallas as pl
import jax.experimental.pallas.tpu as pltpu

bf = jnp.bfloat16
f32 = jnp.float32
LOG2E = 1.4426950408889634
NT = (((1,), (1,)), ((), ()))
TN = (((0,), (0,)), ((), ()))
MESH = pl.DeviceIdType.MESH
R = 1024
D = 768
K = 256
G = 6
GM = 16
CH = 256
NC = R // CH
DB, DC, SLOTS = 5, 10, 12
NX, NY, NZ, NA = 4, 4, 8, 16
ROWS = 262144


def prep(rows, cells, base, cent, rot, wait_rot, residT, yx, yT):
    for b in range(NC):
        rs = slice(b * 256, (b + 1) * 256)
        hot = [
            (lax.broadcasted_iota(jnp.int32, (K, 128), 0) + base == cells[b * 2 + i : b * 2 + i + 1, :]).astype(bf)
            for i in range(2)
        ]
        c = lax.dot_general(jnp.concatenate(hot, axis=1), cent[...], TN, preferred_element_type=f32)
        resid = (rows[rs, :].astype(f32) - c).astype(bf)
        residT[:, rs] = resid.T
        if b == 0:
            wait_rot()
        y = jnp.dot(resid, rot[...], preferred_element_type=f32).astype(bf)
        yT[:, rs] = y.T
        for g in range(G):
            yx[g, rs, :] = y[:, g * 128 : (g + 1) * 128]


def group(g, cb, yx, yT, slots, valid, apT, part, pm, middle):
    U = GM * NC
    mats, lhs, held, sums, mrows = {}, {}, {}, {}, []

    def scores(u):
        j, ch = divmod(u, NC)
        rs = slice(ch * CH, (ch + 1) * CH)
        if ch == 0:
            c = cb[g * GM + j].astype(f32)
            bias = -0.5 * jnp.sum(c * c, axis=0, keepdims=True)
            row = lax.broadcasted_iota(jnp.int32, (128, K), 0)
            mat = jnp.where(row // 8 == j, jnp.concatenate([c] * 16, axis=0), 0.0).astype(bf)
            one = (lax.broadcasted_iota(jnp.int32, (8, K), 0) == 0).astype(f32)
            mats[j] = (mat, jnp.concatenate([c, one], axis=0).astype(bf), bias)
        s = jnp.dot(yx[g, rs, :], mats[j][0], preferred_element_type=f32) + mats[j][2]
        s = s - jnp.max(s, axis=1, keepdims=True)
        slots[u % SLOTS][...] = jnp.exp2(s * LOG2E).astype(bf)

    def reconstruct(u):
        j, ch = divmod(u, NC)
        rs = slice(ch * CH, (ch + 1) * CH)
        q = lax.dot_general(mats[j][1], slots[u % SLOTS][...], NT, preferred_element_type=f32)
        inv = valid[:, rs] / q[8:9, :]
        held[j, ch] = q[0:8, :] * inv
        r0 = pl.multiple_of(g * 128 + (j // 2) * 16, 16)
        y = yT[pl.ds(r0, 16), rs].astype(f32)[(j % 2) * 8 : (j % 2) * 8 + 8, :]
        row = lax.broadcasted_iota(jnp.int32, (8, CH), 0)
        lhs[u] = jnp.concatenate([y * inv, jnp.where(row == 0, inv, 0.0)], axis=0).astype(bf)
        if j % 2 == 1:
            both = [held.pop((j - 1, ch)), held.pop((j, ch))]
            apT[(j // 2) * 16 : (j // 2) * 16 + 16, rs] = jnp.concatenate(both, axis=0).astype(bf)

    def accumulate(u):
        j, ch = divmod(u, NC)
        o = jnp.dot(lhs.pop(u), slots[u % SLOTS][...], preferred_element_type=f32)
        sums[j] = o if ch == 0 else sums[j] + o
        if ch == NC - 1:
            o = sums.pop(j)
            cc, a = j // 8, (j % 8) * 2
            part[g, cc, a, 3] = o[0:8, 0:128]
            part[g, cc, a + 1, 3] = o[0:8, 128:256]
            mrows.append(o[8:9, :])
            if j % 8 == 7:
                m = jnp.concatenate(mrows[-8:], axis=0)
                pm[0, g * 2 + cc] = m[:, 0:128]
                pm[1, g * 2 + cc] = m[:, 128:256]

    for t in range(U + DC):
        if t == U // 2:
            middle()
        if t < U:
            scores(t)
        if 0 <= t - DB < U:
            reconstruct(t - DB)
        if 0 <= t - DC < U:
            accumulate(t - DC)


def covariance(g, residT, apT, part):
    for cc in range(2):
        for hh in range(2):
            i0 = cc * 384 + hh * 192
            v = lax.dot_general(residT[i0 : i0 + 192, :], apT[...], NT, preferred_element_type=f32)
            part[g, cc, hh * 8 : hh * 8 + 8, 0:3] = v.reshape(8, 3, 8, 128)


def kernel(tiles, rows, cells, cent, rot_hbm, cb_hbm, cov_hbm, sums_hbm, mass_hbm,
           rot, cb, cov, sums, mass, residT, yx, yT, apT, part, pm, rc, rcm, sa, ra, rz, out,
           s_in, s_out, s_core, r_core, s_m, r_m, s_a, r_a, s_z, r_z, s_g, r_g, s_c, r_c, *slots):
    grp = lax.axis_index("grp")
    dev = lax.axis_index("dev")
    yy = grp // 2
    c = lax.rem(grp, 2)
    zz = dev // NX
    xx = lax.rem(dev, NX)
    me = yy * NX + xx
    sib = (yy * 2 + 1 - c, dev)

    def plane(a):
        return ((a // NX) * 2 + c, zz * NX + lax.rem(a, NX))

    def column(z):
        return (grp, z * NX + xx)

    others = [lax.rem(me + k, NA) for k in range(1, NA)]
    above = [lax.rem(zz + k, NZ) for k in range(1, NZ)]
    barrier = pltpu.get_barrier_semaphore()
    peers = [sib] + [plane(a) for a in others] + [column(z) for z in above]
    for p in peers:
        pl.semaphore_signal(barrier, inc=1, device_id=p, device_id_type=MESH)

    def copy(src, dst, ss, rs, to):
        return pltpu.make_async_remote_copy(
            src_ref=src, dst_ref=dst, send_sem=ss, recv_sem=rs, device_id=to, device_id_type=MESH
        )

    def size(last):
        return (5, 48) if last else (4, 32)

    def to_out(g):
        cols = pl.ds(pl.multiple_of(g * 128, 128), 128)
        subs = pl.ds(pl.multiple_of(g * GM, GM), GM)
        return (
            pltpu.make_async_copy(cov.at[:, cols], cov_hbm.at[:, cols], s_out.at[0, g]),
            pltpu.make_async_copy(sums.at[subs], sums_hbm.at[subs], s_out.at[1, g]),
        )

    def step(k, g, last=False):
        n, nb = size(last)
        if k == 0:
            copy(part.at[g, 1 - c], rc.at[g], s_core.at[g], r_core.at[g], sib).start()
            if last:
                copy(pm.at[1 - c], rcm, s_m.at[0], r_m.at[0], sib).start()
        if k == 1:
            copy(rc.at[g], rc.at[g], s_core.at[g], r_core.at[g], sib).wait_recv()
            if last:
                copy(rcm, rcm, s_m.at[0], r_m.at[0], sib).wait_recv()
                tot = (pm[c] + rcm[...]).reshape(NA, 8, 128)
                tot = jnp.concatenate([tot, jnp.zeros((NA, 8, 128), f32)], axis=1)
                sa[g, :, 32:48] = tot.astype(bf)
            tot = (part[g, c] + rc[g]).reshape(NA, 32, 128)
            sa[g, :, 0:32] = tot.astype(bf)
            for a in others:
                copy(sa.at[g, a, 0:nb], ra.at[g, me, 0:nb], s_a.at[g], r_a.at[g], plane(a)).start()
            ra[g, me, 0:nb] = sa[g, me, 0:nb]
        if k == 2:
            copy(sa.at[g, 0:15, 0:nb], ra.at[g, 0:15, 0:nb], s_a.at[g], r_a.at[g], sib).wait_recv()
            t = [ra[g, a, 0:nb].astype(f32) for a in range(NA)]
            while len(t) > 1:
                t = [t[i] + t[i + 1] for i in range(0, len(t), 2)]
            rz[g, zz, 0:n] = t[0][0 : n * 8].reshape(n, 8, 128)
            for z in above:
                copy(rz.at[g, zz, 0:n], rz.at[g, zz, 0:n], s_z.at[g], r_z.at[g], column(z)).start()
        if k == 3:
            copy(rz.at[g, 0:7, 0:n], rz.at[g, 0:7, 0:n], s_z.at[g], r_z.at[g], sib).wait_recv()
            t = [rz[g, z, 0:n] for z in range(NZ)]
            while len(t) > 1:
                t = [t[i] + t[i + 1] for i in range(0, len(t), 2)]
            mine = out.at[g, c, me, 0:n]
            mine[...] = t[0]
            for a in others:
                copy(mine, mine, s_g.at[g], r_g.at[g], plane(a)).start()
        if k == 4:
            copy(out.at[g, c, 0:15, 0:n], out.at[g, c, 0:15, 0:n], s_g.at[g], r_g.at[g], sib).wait_recv()
            half = out.at[g, c, :, 0:n]
            copy(half, half, s_c.at[g], r_c.at[g], sib).start()
        if k == 5:
            half = out.at[g, 1 - c, :, 0:n]
            copy(half, half, s_c.at[g], r_c.at[g], sib).wait_recv()
            for cc in range(2):
                i0 = cc * 384
                v = out[g, cc, :, 0:3].reshape(384, 128) * (1.0 / ROWS)
                cov[i0 : i0 + 384, pl.ds(pl.multiple_of(g * 128, 128), 128)] = v
                for a in range(NA):
                    w = a % 2
                    sums[g * GM + cc * 8 + a // 2, :, w * 128 : (w + 1) * 128] = out[g, cc, a, 3] * (K / ROWS)
                if last:
                    for a in range(12):
                        mass[a * 8 : a * 8 + 8, cc * 128 : (cc + 1) * 128] = out[g, cc, a, 4] * (K / ROWS)
            for cp in to_out(g):
                cp.start()

    get_rot = pltpu.make_async_copy(rot_hbm, rot, s_in.at[0])
    get_cb = pltpu.make_async_copy(cb_hbm, cb, s_in.at[1])
    get_rot.start()
    get_cb.start()
    pm[...] = jnp.zeros_like(pm)
    prep(rows, cells, (grp * (NX * NZ) + dev) * K, cent, rot, get_rot.wait, residT, yx, yT)
    pos = lax.broadcasted_iota(jnp.int32, (1, R), 1)
    valid = (pos < jnp.where(pos < 512, tiles[0], 512 + tiles[1])).astype(f32)
    get_cb.wait()

    def when(g, back, k):
        @pl.when(g >= back)
        def _():
            step(k, g - back)

    def body(g, _):
        def middle():
            @pl.when(g == 0)
            def _():
                pl.semaphore_wait(barrier, len(peers))

            when(g, 1, 1)
            when(g, 2, 2)
            when(g, 5, 4)

        group(g, cb, yx, yT, slots, valid, apT, part, pm, middle)
        covariance(g, residT, apT, part)
        step(0, g)
        when(g, 3, 3)
        when(g, 5, 5)
        return 0

    lax.fori_loop(0, G, body, 0)
    copy(pm.at[1 - c], rcm, s_m.at[0], r_m.at[0], sib).start()
    order = ((1, 5), (4, 1), (2, 4), (3, 3), (2, 5), (5, 1), (4, 2), (3, 4), (5, 2), (4, 3), (3, 5), (5, 3), (4, 4), (5, 4), (4, 5), (5, 5))
    for k, g in order:
        step(k, g, g == G - 1)
    put_mass = pltpu.make_async_copy(mass, mass_hbm, s_in.at[0])
    put_mass.start()
    copy(rcm, rcm, s_m.at[0], r_m.at[0], sib).wait_send()
    for g in range(G):
        n, nb = size(g == G - 1)
        copy(rc.at[g], rc.at[g], s_core.at[g], r_core.at[g], sib).wait_send()
        copy(sa.at[g, 0:15, 0:nb], ra.at[g, 0:15, 0:nb], s_a.at[g], r_a.at[g], sib).wait_send()
        copy(rz.at[g, 0:7, 0:n], rz.at[g, 0:7, 0:n], s_z.at[g], r_z.at[g], sib).wait_send()
        copy(out.at[g, 0, 0:15, 0:n], out.at[g, 0, 0:15, 0:n], s_g.at[g], r_g.at[g], sib).wait_send()
        copy(out.at[g, 0, :, 0:n], out.at[g, 0, :, 0:n], s_c.at[g], r_c.at[g], sib).wait_send()
        for cp in to_out(g):
            cp.wait()
    put_mass.wait()


def run(tiles, rows, cells, cent, rot, cb):
    V = pl.BlockSpec(memory_space=pltpu.VMEM)
    A = pl.BlockSpec(memory_space=pl.ANY)
    S = jax.ShapeDtypeStruct
    VM = pltpu.VMEM
    DS = pltpu.SemaphoreType.DMA

    def T(*n):
        return VM(n + (8, 128), f32)

    return pl.pallas_call(
        kernel,
        out_shape=(S((D, D), f32), S((96, 8, K), f32), S((96, K), f32)),
        in_specs=[pl.BlockSpec(memory_space=pltpu.SMEM), V, V, V, A, A],
        out_specs=(A, A, A),
        scratch_shapes=[
            VM((D, D), bf), VM((96, 8, K), bf), VM((D, D), f32), VM((96, 8, K), f32), VM((96, K), f32),
            VM((D, R), bf), VM((G, R, 128), bf), VM((D, R), bf), VM((128, R), bf),
            T(G, 2, NA, 4), T(2, NA), T(G, NA, 4), T(NA),
            VM((G, NA, 48, 128), bf), VM((G, NA, 48, 128), bf), T(G, NZ, 5), T(G, 2, NA, 5),
            DS((2,)), DS((2, G)), DS((G,)), DS((G,)), DS((1,)), DS((1,)), DS((G,)), DS((G,)),
            DS((G,)), DS((G,)), DS((G,)), DS((G,)), DS((G,)), DS((G,)),
        ] + [VM((CH, K), bf)] * SLOTS,
        compiler_params=pltpu.CompilerParams(vmem_limit_bytes=56 * 2**20, collective_id=0, has_side_effects=True),
        cost_estimate=pl.CostEstimate(flops=2**34, bytes_accessed=2**23, transcendentals=2**24),
    )(tiles, rows, cells, cent, rot, cb)


def per_device(sample_rows, row_cell, tile_rows, centroids, rotation, codebooks):
    return run(tile_rows, sample_rows, row_cell.reshape(8, 128), centroids, rotation, codebooks)


def solution(mesh):
    placed = (P(("grp", "dev"), None), P(("grp", "dev")), P(("grp", "dev")), P(("grp", "dev"), None), P(), P())
    return jax.shard_map(
        per_device, mesh=mesh, in_specs=placed, out_specs=(P(), P(), P()), check_vma=False
    )
```

```python
import functools
import jax
import jax.numpy as jnp
from jax import lax
from jax.sharding import PartitionSpec as P
import jax.experimental.pallas as pl
import jax.experimental.pallas.tpu as pltpu

bf = jnp.bfloat16
f32 = jnp.float32
LOG2E = 1.4426950408889634
NT = (((1,), (1,)), ((), ()))
TN = (((0,), (0,)), ((), ()))
MESH = pl.DeviceIdType.MESH
R = 1024
D = 768
K = 256
G = 6
GM = 16
CH = 256
NC = R // CH
CHB = 512
NCB = R // CHB
PB = CHB // CH
DB, DC, SLOTS = 6, 12, 6
NX, NY, NZ, NA = 4, 4, 8, 16
ROWS = 262144
VL = 52


def prep(rows, cells, base, cent, rot, rows_of, wait_rot, resid, yx, yT):
    for b in range(NC):
        rs = slice(b * 256, (b + 1) * 256)
        hot = [
            (lax.broadcasted_iota(jnp.int32, (K, 128), 0) + base == cells[b * 2 + i : b * 2 + i + 1, :]).astype(bf)
            for i in range(2)
        ]
        c = lax.dot_general(jnp.concatenate(hot, axis=1), cent[...], TN, preferred_element_type=f32)
        rows_of(b).wait()
        r = (rows[rs, :].astype(f32) - c).astype(bf)
        resid[rs, :] = r
        if b == 0:
            wait_rot()
        y = jnp.dot(r, rot[...], preferred_element_type=f32).astype(bf)
        yT[:, rs] = y.T
        for g in range(G):
            yx[g, rs, :] = y[:, g * 128 : (g + 1) * 128]


def group(g, cb, yx, yT, slots, valid, apT, part, pm, middle):
    U = GM * NC
    mats, lhs, held, sums, mrows = {}, {}, {}, {}, []

    def scores(u):
        j, ch = divmod(u, NC)
        rs = slice(ch * CH, (ch + 1) * CH)
        if ch == 0:
            c = cb[g * GM + j].astype(f32)
            bias = -0.5 * jnp.sum(c * c, axis=0, keepdims=True)
            row = lax.broadcasted_iota(jnp.int32, (128, K), 0)
            mat = jnp.where(row // 8 == j, jnp.concatenate([c] * 16, axis=0), 0.0).astype(bf)
            one = (lax.broadcasted_iota(jnp.int32, (8, K), 0) == 0).astype(f32)
            mats[j] = (mat, jnp.concatenate([c, one], axis=0).astype(bf), bias)
        s = jnp.dot(yx[g, rs, :], mats[j][0], preferred_element_type=f32) + mats[j][2]
        s = s - jnp.max(s, axis=1, keepdims=True)
        slots[j % SLOTS][rs, :] = jnp.exp2(s * LOG2E).astype(bf)

    def reconstruct(u):
        j, ch = divmod(u, NCB)
        rs = slice(ch * CHB, (ch + 1) * CHB)
        q = lax.dot_general(mats[j][1], slots[j % SLOTS][rs, :], NT, preferred_element_type=f32)
        inv = valid[:, rs] / q[8:9, :]
        held[j, ch] = q[0:8, :] * inv
        r0 = pl.multiple_of(g * 128 + (j // 2) * 16, 16)
        y = yT[pl.ds(r0, 16), rs].astype(f32)[(j % 2) * 8 : (j % 2) * 8 + 8, :]
        row = lax.broadcasted_iota(jnp.int32, (8, CHB), 0)
        lhs[u] = jnp.concatenate([y * inv, jnp.where(row == 0, inv, 0.0)], axis=0).astype(bf)
        if j % 2 == 1:
            both = [held.pop((j - 1, ch)), held.pop((j, ch))]
            apT[(j // 2) * 16 : (j // 2) * 16 + 16, rs] = jnp.concatenate(both, axis=0).astype(bf)

    def accumulate(u):
        j, ch = divmod(u, NCB)
        rs = slice(ch * CHB, (ch + 1) * CHB)
        o = jnp.dot(lhs.pop(u), slots[j % SLOTS][rs, :], preferred_element_type=f32)
        sums[j] = o if ch == 0 else sums[j] + o
        if ch == NCB - 1:
            o = sums.pop(j)
            cc, a = j // 8, (j % 8) * 2
            part[g, cc, a, 3] = o[0:8, 0:128]
            part[g, cc, a + 1, 3] = o[0:8, 128:256]
            mrows.append(o[8:9, :])
            if j % 8 == 7:
                m = jnp.concatenate(mrows[-8:], axis=0)
                pm[0, g * 2 + cc] = m[:, 0:128]
                pm[1, g * 2 + cc] = m[:, 128:256]

    for t in range(U + DC):
        if t == U // 2:
            middle()
        if t < U:
            scores(t)
        if 0 <= t - DB < U and (t - DB) % PB == PB - 1:
            reconstruct((t - DB) // PB)
        if 0 <= t - DC < U and (t - DC) % PB == PB - 1:
            accumulate((t - DC) // PB)


def covariance(g, resid, apT, part):
    v = jnp.dot(apT[...], resid[...], preferred_element_type=f32)
    for cc in range(2):
        part[g, cc, :, 0:3] = v[:, cc * 384 : cc * 384 + 384].T.reshape(NA, 3, 8, 128)


def kernel(tiles, cells, rows_hbm, cent_hbm, rot_hbm, cb_hbm, cov, sums, mass,
           rows, cent, rot, cb, resid, yx, yT, apT, part, pm, rc, rcm, sa, ra, rz, out,
           s_in, s_core, r_core, s_m, r_m, s_a, r_a, s_z, r_z, s_g, r_g, s_c, r_c, *slots):
    grp = lax.axis_index("grp")
    dev = lax.axis_index("dev")
    yy = grp // 2
    c = lax.rem(grp, 2)
    zz = dev // NX
    xx = lax.rem(dev, NX)
    me = yy * NX + xx
    sib = (yy * 2 + 1 - c, dev)

    def plane(a):
        return ((a // NX) * 2 + c, zz * NX + lax.rem(a, NX))

    def column(z):
        return (grp, z * NX + xx)

    others = [lax.rem(me + k, NA) for k in range(1, NA)]
    above = [lax.rem(zz + k, NZ) for k in range(1, NZ)]
    def copy(src, dst, ss, rs, to):
        return pltpu.make_async_remote_copy(
            src_ref=src, dst_ref=dst, send_sem=ss, recv_sem=rs, device_id=to, device_id_type=MESH
        )

    def size(last):
        return (5, 48) if last else (4, 32)

    def step(k, g, last=False):
        n, nb = size(last)
        if k == 0:
            copy(part.at[g, 1 - c], rc.at[g], s_core.at[g], r_core.at[g], sib).start()
            if last:
                copy(pm.at[1 - c], rcm, s_m.at[0], r_m.at[0], sib).start()
        if k == 1:
            copy(rc.at[g], rc.at[g], s_core.at[g], r_core.at[g], sib).wait_recv()
            if last:
                copy(rcm, rcm, s_m.at[0], r_m.at[0], sib).wait_recv()
                tot = (pm[c] + rcm[...]).reshape(NA, 8, 128)
                tot = jnp.concatenate([tot, jnp.zeros((NA, 8, 128), f32)], axis=1)
                sa[g, :, 32:48] = tot.astype(bf)
            tot = (part[g, c] + rc[g]).reshape(NA, 32, 128)
            sa[g, :, 0:32] = tot.astype(bf)
            for a in others:
                copy(sa.at[g, a, 0:nb], ra.at[g, me, 0:nb], s_a.at[g], r_a.at[g], plane(a)).start()
            ra[g, me, 0:nb] = sa[g, me, 0:nb]
        if k == 2:
            copy(sa.at[g, 0:15, 0:nb], ra.at[g, 0:15, 0:nb], s_a.at[g], r_a.at[g], sib).wait_recv()
            t = [ra[g, a, 0:nb].astype(f32) for a in range(NA)]
            while len(t) > 1:
                t = [t[i] + t[i + 1] for i in range(0, len(t), 2)]
            rz[g, zz, 0:n] = t[0][0 : n * 8].reshape(n, 8, 128)
            for z in above:
                copy(rz.at[g, zz, 0:n], rz.at[g, zz, 0:n], s_z.at[g], r_z.at[g], column(z)).start()
        if k == 3:
            copy(rz.at[g, 0:7, 0:n], rz.at[g, 0:7, 0:n], s_z.at[g], r_z.at[g], sib).wait_recv()
            t = [rz[g, z, 0:n] for z in range(NZ)]
            while len(t) > 1:
                t = [t[i] + t[i + 1] for i in range(0, len(t), 2)]
            mine = out.at[g, c, me, 0:n]
            mine[...] = t[0]
            for a in others:
                copy(mine, mine, s_g.at[g], r_g.at[g], plane(a)).start()
        if k == 4:
            copy(out.at[g, c, 0:15, 0:n], out.at[g, c, 0:15, 0:n], s_g.at[g], r_g.at[g], sib).wait_recv()
            half = out.at[g, c, :, 0:n]
            copy(half, half, s_c.at[g], r_c.at[g], sib).start()
        if k == 5:
            half = out.at[g, 1 - c, :, 0:n]
            copy(half, half, s_c.at[g], r_c.at[g], sib).wait_recv()
            for cc in range(2):
                i0 = cc * 384
                v = out[g, cc, :, 0:3].reshape(384, 128) * (1.0 / ROWS)
                cov[i0 : i0 + 384, pl.ds(pl.multiple_of(g * 128, 128), 128)] = v
                for a in range(NA):
                    w = a % 2
                    sums[g * GM + cc * 8 + a // 2, :, w * 128 : (w + 1) * 128] = out[g, cc, a, 3] * (K / ROWS)
                if last:
                    for a in range(12):
                        mass[a * 8 : a * 8 + 8, cc * 128 : (cc + 1) * 128] = out[g, cc, a, 4] * (K / ROWS)

    barrier = pltpu.get_barrier_semaphore()
    peers = [sib] + [plane(a) for a in others] + [column(z) for z in above]
    for p in peers:
        pl.semaphore_signal(barrier, inc=1, device_id=p, device_id_type=MESH)

    def rows_of(b):
        rs = slice(b * 256, (b + 1) * 256)
        return pltpu.make_async_copy(rows_hbm.at[rs], rows.at[rs], s_in.at[3 + b])

    get_cent = pltpu.make_async_copy(cent_hbm, cent, s_in.at[2])
    get_rot = pltpu.make_async_copy(rot_hbm, rot, s_in.at[0])
    get_cb = pltpu.make_async_copy(cb_hbm, cb, s_in.at[1])
    for cp in [get_cent, rows_of(0), get_rot] + [rows_of(b) for b in range(1, NC)] + [get_cb]:
        cp.start()
    pm[...] = jnp.zeros_like(pm)
    get_cent.wait()
    prep(rows, cells, (grp * (NX * NZ) + dev) * K, cent, rot, rows_of, get_rot.wait, resid, yx, yT)
    pos = lax.broadcasted_iota(jnp.int32, (1, R), 1)
    valid = (pos < jnp.where(pos < 512, tiles[0], 512 + tiles[1])).astype(f32)
    get_cb.wait()

    def when(g, back, k):
        @pl.when(g >= back)
        def _():
            step(k, g - back)

    def body(g, _):
        def middle():
            @pl.when(g == 0)
            def _():
                pl.semaphore_wait(barrier, len(peers))

            when(g, 1, 1)
            when(g, 2, 2)
            when(g, 5, 4)

        group(g, cb, yx, yT, slots, valid, apT, part, pm, middle)
        covariance(g, resid, apT, part)
        step(0, g)
        when(g, 3, 3)
        when(g, 5, 5)
        return 0

    lax.fori_loop(0, G, body, 0)
    copy(pm.at[1 - c], rcm, s_m.at[0], r_m.at[0], sib).start()
    order = ((1, 5), (4, 1), (2, 4), (3, 3), (2, 5), (5, 1), (4, 2), (3, 4), (5, 2), (4, 3), (3, 5), (5, 3), (4, 4), (5, 4), (4, 5), (5, 5))
    for k, g in order:
        step(k, g, g == G - 1)
    copy(rcm, rcm, s_m.at[0], r_m.at[0], sib).wait_send()
    for g in range(G):
        n, nb = size(g == G - 1)
        copy(rc.at[g], rc.at[g], s_core.at[g], r_core.at[g], sib).wait_send()
        copy(sa.at[g, 0:15, 0:nb], ra.at[g, 0:15, 0:nb], s_a.at[g], r_a.at[g], sib).wait_send()
        copy(rz.at[g, 0:7, 0:n], rz.at[g, 0:7, 0:n], s_z.at[g], r_z.at[g], sib).wait_send()
        copy(out.at[g, 0, 0:15, 0:n], out.at[g, 0, 0:15, 0:n], s_g.at[g], r_g.at[g], sib).wait_send()
        copy(out.at[g, 0, :, 0:n], out.at[g, 0, :, 0:n], s_c.at[g], r_c.at[g], sib).wait_send()


def run(tiles, rows, cells, cent, rot, cb):
    V = pl.BlockSpec(memory_space=pltpu.VMEM)
    A = pl.BlockSpec(memory_space=pltpu.HBM)
    VM = pltpu.VMEM
    DS = pltpu.SemaphoreType.DMA

    def T(*n):
        return VM(n + (8, 128), f32)

    return pl.pallas_call(
        kernel,
        out_shape=(VM((D, D), f32), VM((96, 8, K), f32), VM((96, K), f32)),
        in_specs=[pl.BlockSpec(memory_space=pltpu.SMEM), V, A, A, A, A],
        out_specs=(V, V, V),
        scratch_shapes=[
            VM((R, D), bf), VM((K, D), bf), VM((D, D), bf), VM((96, 8, K), bf),
            VM((R, D), bf), VM((G, R, 128), bf), VM((D, R), bf), VM((128, R), bf),
            T(G, 2, NA, 4), T(2, NA), T(G, NA, 4), T(NA),
            VM((G, NA, 48, 128), bf), VM((G, NA, 48, 128), bf), T(G, NZ, 5), T(G, 2, NA, 5),
            DS((7,)), DS((G,)), DS((G,)), DS((1,)), DS((1,)), DS((G,)), DS((G,)),
            DS((G,)), DS((G,)), DS((G,)), DS((G,)), DS((G,)), DS((G,)),
        ] + [VM((R, K), bf)] * SLOTS,
        compiler_params=pltpu.CompilerParams(vmem_limit_bytes=VL * 2**20, collective_id=0, has_side_effects=True),
        cost_estimate=pl.CostEstimate(flops=2**34, bytes_accessed=2**23, transcendentals=2**24),
    )(tiles, cells, rows, cent, rot, cb)


def per_device(sample_rows, row_cell, tile_rows, centroids, rotation, codebooks):
    return run(tile_rows, sample_rows, row_cell.reshape(8, 128), centroids, rotation, codebooks)


def solution(mesh):
    placed = (P(("grp", "dev"), None), P(("grp", "dev")), P(("grp", "dev")), P(("grp", "dev"), None), P(), P())
    return jax.shard_map(
        per_device, mesh=mesh, in_specs=placed, out_specs=(P(), P(), P()), check_vma=False
    )
```

```python
import functools
import jax
import jax.numpy as jnp
from jax import lax
from jax.sharding import PartitionSpec as P
import jax.experimental.pallas as pl
import jax.experimental.pallas.tpu as pltpu

bf = jnp.bfloat16
f32 = jnp.float32
LOG2E = 1.4426950408889634
NT = (((1,), (1,)), ((), ()))
TN = (((0,), (0,)), ((), ()))
MESH = pl.DeviceIdType.MESH
R = 1024
D = 768
K = 256
G = 6
GM = 16
CH = 256
NC = R // CH
CHB = 512
NCB = R // CHB
PB = CHB // CH
DB, DC, SLOTS = 6, 12, 8
U = GM * NC
Q = G + 1
NX, NY, NZ, NA = 4, 4, 8, 16
ROWS = 262144
VL = 52


def prep(rows, cells, base, cent, rot, rows_of, wait_rot, resid, yx, yT):
    for b in range(NC):
        rs = slice(b * 256, (b + 1) * 256)
        hot = [
            (lax.broadcasted_iota(jnp.int32, (K, 128), 0) + base == cells[b * 2 + i : b * 2 + i + 1, :]).astype(bf)
            for i in range(2)
        ]
        c = lax.dot_general(jnp.concatenate(hot, axis=1), cent[...], TN, preferred_element_type=f32)
        rows_of(b).wait()
        r = (rows[rs, :].astype(f32) - c).astype(bf)
        resid[rs, :] = r
        if b == 0:
            wait_rot()
        y = jnp.dot(r, rot[...], preferred_element_type=f32).astype(bf)
        yT[:, rs] = y.T
        for g in range(G):
            yx[g, rs, :] = y[:, g * 128 : (g + 1) * 128]


def scores(t, g, cb, yx, mats, slots):
    j, ch = divmod(t, NC)
    rs = slice(ch * CH, (ch + 1) * CH)
    if ch == 0:
        c = cb[g * GM + j].astype(f32)
        bias = -0.5 * jnp.sum(c * c, axis=0, keepdims=True)
        row = lax.broadcasted_iota(jnp.int32, (128, K), 0)
        mats[j] = (jnp.where(row // 8 == j, jnp.concatenate([c] * 16, axis=0), 0.0).astype(bf), bias)
    s = jnp.dot(yx[g, rs, :], mats[j][0], preferred_element_type=f32) + mats[j][1]
    s = s - jnp.max(s, axis=1, keepdims=True)
    slots[j % SLOTS][rs, :] = jnp.exp2(s * LOG2E).astype(bf)


def reconstruct(u, g, cb, yT, valid, slots, held, lhs, apT):
    j, ch = divmod(u, NCB)
    rs = slice(ch * CHB, (ch + 1) * CHB)
    one = (lax.broadcasted_iota(jnp.int32, (8, K), 0) == 0).astype(f32)
    mat = jnp.concatenate([cb[g * GM + j].astype(f32), one], axis=0).astype(bf)
    q = lax.dot_general(mat, slots[j % SLOTS][rs, :], NT, preferred_element_type=f32)
    inv = valid[:, rs] / q[8:9, :]
    r0 = pl.multiple_of(g * 128 + (j // 2) * 16, 16)
    y = yT[pl.ds(r0, 16), rs].astype(f32)[(j % 2) * 8 : (j % 2) * 8 + 8, :]
    row = lax.broadcasted_iota(jnp.int32, (8, CHB), 0)
    lhs[u % 8] = jnp.concatenate([y * inv, jnp.where(row == 0, inv, 0.0)], axis=0).astype(bf)
    if j % 2 == 0:
        held[ch] = q[0:8, :] * inv
    else:
        apT[(j // 2) * 16 : (j // 2) * 16 + 16, rs] = jnp.concatenate([held[ch], q[0:8, :] * inv], axis=0).astype(bf)


def accumulate(u, g, slots, lhs, acc, mrow, part, pm):
    j, ch = divmod(u, NCB)
    rs = slice(ch * CHB, (ch + 1) * CHB)
    o = jnp.dot(lhs[u % 8], slots[j % SLOTS][rs, :], preferred_element_type=f32)
    if ch == 0:
        acc[j % 2] = o
    else:
        o = acc[j % 2] + o
        cc, a = j // 8, (j % 8) * 2
        part[g, cc, a, 3] = o[0:8, 0:128]
        part[g, cc, a + 1, 3] = o[0:8, 128:256]
        mrow[j % 8 : j % 8 + 1, :] = o[8:9, :]
        if j % 8 == 7:
            pm[0, g * 2 + cc] = mrow[:, 0:128]
            pm[1, g * 2 + cc] = mrow[:, 128:256]


def covariance(g, resid, apT, part):
    v = jnp.dot(apT[...], resid[...], preferred_element_type=f32)
    for cc in range(2):
        part[g, cc, :, 0:3] = v[:, cc * 384 : cc * 384 + 384].T.reshape(NA, 3, 8, 128)


def half_group(e, resid, apT, part, ph):
    v = jnp.dot(apT[e * 64 : e * 64 + 64, :], resid[...], preferred_element_type=f32)
    v = jnp.concatenate([v[:, 0:384], v[:, 384:768]], axis=0).T
    for cc in range(2):
        ph[e, cc, 0:12] = v[cc * 192 : cc * 192 + 192].reshape(12, 2, 8, 128)
        for a in range(8):
            ph[e, cc, 12 + a // 2, a % 2] = part[G - 1, e, cc * 8 + a, 3]


def kernel(tiles, cells, rows_hbm, cent_hbm, rot_hbm, cb_hbm, cov, sums, mass,
           rows, cent, rot, cb, resid, yx, yT, apT, held, lhs, acc, mrow, part, ph, pm, rc, rcm, sa, ra, rz, out,
           s_in, s_core, r_core, s_m, r_m, s_a, r_a, s_z, r_z, s_g, r_g, s_c, r_c, *slots):
    grp = lax.axis_index("grp")
    dev = lax.axis_index("dev")
    yy = grp // 2
    c = lax.rem(grp, 2)
    zz = dev // NX
    xx = lax.rem(dev, NX)
    me = yy * NX + xx
    sib = (yy * 2 + 1 - c, dev)

    def plane(a):
        return ((a // NX) * 2 + c, zz * NX + lax.rem(a, NX))

    def column(z):
        return (grp, z * NX + xx)

    others = [lax.rem(me + k, NA) for k in range(1, NA)]
    above = [lax.rem(zz + k, NZ) for k in range(1, NZ)]
    def copy(src, dst, ss, rs, to):
        return pltpu.make_async_remote_copy(
            src_ref=src, dst_ref=dst, send_sem=ss, recv_sem=rs, device_id=to, device_id_type=MESH
        )

    def size(kind):
        return ((4, 4, 32), (2, 2, 16), (2, 3, 32))[kind]

    def step(k, q, kind=0):
        m, n, nb = size(kind)
        mine_of, from_sib = (part.at[q, c], part.at[q, 1 - c]) if kind == 0 else (ph.at[kind - 1, c], ph.at[kind - 1, 1 - c])
        got = rc.at[q, :, 0:m]
        if k == 0:
            copy(from_sib, got, s_core.at[q], r_core.at[q], sib).start()
            if kind == 2:
                copy(pm.at[1 - c], rcm, s_m.at[0], r_m.at[0], sib).start()
        if k == 1:
            copy(got, got, s_core.at[q], r_core.at[q], sib).wait_recv()
            if kind == 2:
                copy(rcm, rcm, s_m.at[0], r_m.at[0], sib).wait_recv()
                tot = (pm[c] + rcm[...]).reshape(NA, 8, 128)
                tot = jnp.concatenate([tot, jnp.zeros((NA, 8, 128), f32)], axis=1)
                sa[q, :, 16:32] = tot.astype(bf)
            sa[q, :, 0 : m * 8] = (mine_of[...] + got[...]).reshape(NA, m * 8, 128).astype(bf)
            for a in others:
                copy(sa.at[q, a, 0:nb], ra.at[q, me, 0:nb], s_a.at[q], r_a.at[q], plane(a)).start()
            ra[q, me, 0:nb] = sa[q, me, 0:nb]
        if k == 2:
            copy(sa.at[q, 0:15, 0:nb], ra.at[q, 0:15, 0:nb], s_a.at[q], r_a.at[q], sib).wait_recv()
            t = [ra[q, a, 0:nb].astype(f32) for a in range(NA)]
            while len(t) > 1:
                t = [t[i] + t[i + 1] for i in range(0, len(t), 2)]
            rz[q, zz, 0:n] = t[0][0 : n * 8].reshape(n, 8, 128)
            for z in above:
                copy(rz.at[q, zz, 0:n], rz.at[q, zz, 0:n], s_z.at[q], r_z.at[q], column(z)).start()
        if k == 3:
            copy(rz.at[q, 0:7, 0:n], rz.at[q, 0:7, 0:n], s_z.at[q], r_z.at[q], sib).wait_recv()
            t = [rz[q, z, 0:n] for z in range(NZ)]
            while len(t) > 1:
                t = [t[i] + t[i + 1] for i in range(0, len(t), 2)]
            mine = out.at[q, c, me, 0:n]
            mine[...] = t[0]
            for a in others:
                copy(mine, mine, s_g.at[q], r_g.at[q], plane(a)).start()
        if k == 4:
            copy(out.at[q, c, 0:15, 0:n], out.at[q, c, 0:15, 0:n], s_g.at[q], r_g.at[q], sib).wait_recv()
            half = out.at[q, c, :, 0:n]
            copy(half, half, s_c.at[q], r_c.at[q], sib).start()
            unpack(q, kind, c)
        if k == 5:
            half = out.at[q, 1 - c, :, 0:n]
            copy(half, half, s_c.at[q], r_c.at[q], sib).wait_recv()
            unpack(q, kind, 1 - c)

    def unpack(q, kind, cc):
        if kind == 0:
            v = out[q, cc, :, 0:3].reshape(384, 128) * (1.0 / ROWS)
            cov[pl.ds(pl.multiple_of(cc * 384, 8), 384), pl.ds(pl.multiple_of(q * 128, 128), 128)] = v
            for a in range(NA):
                w = a % 2
                sums[q * GM + cc * 8 + a // 2, :, w * 128 : (w + 1) * 128] = out[q, cc, a, 3] * (K / ROWS)
        else:
            for a in range(8):
                w = a % 2
                i = (G - 1) * GM + (kind - 1) * 8 + cc * 4 + a // 2
                sums[i, :, w * 128 : (w + 1) * 128] = out[q, cc, 12 + a // 2, w] * (K / ROWS)
        if kind == 2:
            i0 = cc * 192
            v0 = out[q - 1, cc, 0:12, 0:2].reshape(192, 128) * (1.0 / ROWS)
            v1 = out[q, cc, 0:12, 0:2].reshape(192, 128) * (1.0 / ROWS)
            low = lax.broadcasted_iota(jnp.int32, (192, 128), 1) < 64
            cov[pl.ds(pl.multiple_of(i0, 8), 192), 640:768] = jnp.where(low, v0, pltpu.roll(v1, 64, 1))
            cov[pl.ds(pl.multiple_of(384 + i0, 8), 192), 640:768] = jnp.where(low, pltpu.roll(v0, 64, 1), v1)
            for a in range(12):
                mass[a * 8 : a * 8 + 8, pl.ds(pl.multiple_of(cc * 128, 128), 128)] = out[q, cc, a, 2] * (K / ROWS)

    barrier = pltpu.get_barrier_semaphore()
    peers = [sib] + [plane(a) for a in others] + [column(z) for z in above]
    for p in peers:
        pl.semaphore_signal(barrier, inc=1, device_id=p, device_id_type=MESH)

    def rows_of(b):
        rs = slice(b * 256, (b + 1) * 256)
        return pltpu.make_async_copy(rows_hbm.at[rs], rows.at[rs], s_in.at[3 + b])

    get_cent = pltpu.make_async_copy(cent_hbm, cent, s_in.at[2])
    get_rot = pltpu.make_async_copy(rot_hbm, rot, s_in.at[0])
    get_cb = pltpu.make_async_copy(cb_hbm, cb, s_in.at[1])
    for cp in [get_cent, rows_of(0), get_rot] + [rows_of(b) for b in range(1, NC)] + [get_cb]:
        cp.start()
    pm[...] = jnp.zeros_like(pm)
    get_cent.wait()
    prep(rows, cells, (grp * (NX * NZ) + dev) * K, cent, rot, rows_of, get_rot.wait, resid, yx, yT)
    pos = lax.broadcasted_iota(jnp.int32, (1, R), 1)
    valid = (pos < jnp.where(pos < 512, tiles[0], 512 + tiles[1])).astype(f32)
    get_cb.wait()

    def when(g, back, k):
        @pl.when(g >= back)
        def _():
            step(k, g - back)

    def later(t, g, before):
        for lag, work in ((DB, recon), (DC, accum)):
            v = t - lag
            if v % PB == PB - 1 and (v < 0 or g is not None):
                work((v % U) // PB, before if v < 0 else g)

    def recon(u, g):
        reconstruct(u, g, cb, yT, valid, slots, held, lhs, apT)

    def accum(u, g):
        accumulate(u, g, slots, lhs, acc, mrow, part, pm)

    def body(g, _):
        before = jnp.maximum(g - 1, 0)
        mats = {}
        for t in range(U):
            scores(t, g, cb, yx, mats, slots)
            later(t, g, before)
            if t == DB:
                covariance(before, resid, apT, part)
            if t == DC:

                @pl.when(g >= 1)
                def _():
                    @pl.when(g == 1)
                    def _():
                        pl.semaphore_wait(barrier, len(peers))

                    step(0, g - 1)
                    when(g, 4, 3)

            if t == U // 2 + DC:

                @pl.when(g >= 1)
                def _():
                    step(1, g - 1)
                    when(g, 2, 2)

                    @pl.when(g == G - 1)
                    def _():
                        half_group(0, resid, apT, part, ph)
                        step(0, G - 1, 1)

        return 0

    lax.fori_loop(0, G, body, 0)
    step(1, 5, 1)
    for t in range(U, U + DC):
        later(t - U, None, G - 1)
    half_group(1, resid, apT, part, ph)
    step(0, 6, 2)
    order = (
        (1, 6), (3, 2), (2, 4), (2, 5), (2, 6), (3, 3), (3, 5), (3, 4), (3, 6), (4, 0), (5, 0), (4, 1), (5, 1),
        (4, 2), (5, 2), (4, 3), (5, 3), (4, 5), (4, 4), (5, 4), (5, 5), (4, 6), (5, 6),
    )
    for k, q in order:
        step(k, q, max(q - 4, 0))
    copy(rcm, rcm, s_m.at[0], r_m.at[0], sib).wait_send()
    for q in range(Q):
        m, n, nb = size(max(q - 4, 0))
        copy(rc.at[q, :, 0:m], rc.at[q, :, 0:m], s_core.at[q], r_core.at[q], sib).wait_send()
        copy(sa.at[q, 0:15, 0:nb], ra.at[q, 0:15, 0:nb], s_a.at[q], r_a.at[q], sib).wait_send()
        copy(rz.at[q, 0:7, 0:n], rz.at[q, 0:7, 0:n], s_z.at[q], r_z.at[q], sib).wait_send()
        copy(out.at[q, 0, 0:15, 0:n], out.at[q, 0, 0:15, 0:n], s_g.at[q], r_g.at[q], sib).wait_send()
        copy(out.at[q, 0, :, 0:n], out.at[q, 0, :, 0:n], s_c.at[q], r_c.at[q], sib).wait_send()


def run(tiles, rows, cells, cent, rot, cb):
    V = pl.BlockSpec(memory_space=pltpu.VMEM)
    A = pl.BlockSpec(memory_space=pltpu.HBM)
    VM = pltpu.VMEM
    DS = pltpu.SemaphoreType.DMA

    def T(*n):
        return VM(n + (8, 128), f32)

    return pl.pallas_call(
        kernel,
        out_shape=(VM((D, D), f32), VM((96, 8, K), f32), VM((96, K), f32)),
        in_specs=[pl.BlockSpec(memory_space=pltpu.SMEM), V, A, A, A, A],
        out_specs=(V, V, V),
        scratch_shapes=[
            VM((R, D), bf), VM((K, D), bf), VM((D, D), bf), VM((96, 8, K), bf),
            VM((R, D), bf), VM((G, R, 128), bf), VM((D, R), bf), VM((128, R), bf),
            VM((NCB, 8, CHB), f32), VM((8, 16, CHB), bf), VM((2, 16, K), f32), VM((8, K), f32),
            T(G, 2, NA, 4), T(2, 2, NA, 2), T(2, NA), T(Q, NA, 4), T(NA),
            VM((Q, NA, 32, 128), bf), VM((Q, NA, 32, 128), bf), T(Q, NZ, 4), T(Q, 2, NA, 4),
            DS((7,)), DS((Q,)), DS((Q,)), DS((1,)), DS((1,)), DS((Q,)), DS((Q,)),
            DS((Q,)), DS((Q,)), DS((Q,)), DS((Q,)), DS((Q,)), DS((Q,)),
        ] + [VM((R, K), bf)] * SLOTS,
        compiler_params=pltpu.CompilerParams(vmem_limit_bytes=VL * 2**20, collective_id=0, has_side_effects=True),
        cost_estimate=pl.CostEstimate(flops=2**34, bytes_accessed=2**23, transcendentals=2**24),
    )(tiles, cells, rows, cent, rot, cb)


def per_device(sample_rows, row_cell, tile_rows, centroids, rotation, codebooks):
    return run(tile_rows, sample_rows, row_cell.reshape(8, 128), centroids, rotation, codebooks)


def solution(mesh):
    placed = (P(("grp", "dev"), None), P(("grp", "dev")), P(("grp", "dev")), P(("grp", "dev"), None), P(), P())
    return jax.shard_map(
        per_device, mesh=mesh, in_specs=placed, out_specs=(P(), P(), P()), check_vma=False
    )
```
